256 devices in a mesh: row: 16 (over x_lo, y, core), col: 16 (over z, x_hi).
Axes of the slice: x: 4 (x_hi: 2, x_lo: 2; x = x_hi * 2 + x_lo), y: 4, z: 8, core: 2. Of those that a mesh axis runs over, the one named last changes fastest.
Arguments:
- amplitudes: bfloat16 [6144, 163840], P('row', 'col'), may hold values from -6 to 6
- integrals: bfloat16 [163840, 1024], P('col', 'row'), may hold values from -0.01953125 to 0.01953125
- pair_first: int32 [1024], P('col'), may hold values from 0 to 1599
- pair_second: int32 [1024], P('col'), may hold values from 0 to 1599
- occ_energy: float32 [200], replicated, may hold values from -1 to -0.5
- vir_energy: float32 [1600], replicated, may hold values from 0.25 to 1
Outputs:
- update: bfloat16 [6144, 1024], P('row', 'col')
The draws below stay inside these ranges and needn't reach their ends.
All inputs are finite; a program needn't handle non-finite values.
Results may differ from the reference program's by a relative error of at most 0.001.
Values may be sent and summed in bfloat16 or wider, within the bound.
No kernel may reach another device: no remote copies, remote signals or barrier semaphores. Data moves between devices by JAX's collectives and lax.ppermute only.
A program may use at most 128 MiB of HBM per device.

```python
import jax
import jax.numpy as jnp

NOCC = 200
NVIR = 1600
CD = 163840
AB = 1024
OO = 6144


def touch_ends(array, stream_key, least, top_value):
    longest = array.shape.index(max(array.shape))
    spots = []
    for shift in (0, 1):
        where = [jax.random.randint(jax.random.fold_in(stream_key, axis), (), 0, length) for axis, length in enumerate(array.shape)]
        where[longest] = (where[longest] + shift) % array.shape[longest]
        spots.append(tuple(where))
    return array.at[spots[0]].set(least).at[spots[1]].set(top_value)


def raised(result, key, source, target, shards_of, factor):
    def block_of(dim):
        return (jnp.arange(result.shape[dim]) // (result.shape[dim] // shards_of)).reshape((-1,) + (1,) * (result.ndim - 1 - dim))

    near = jax.random.permutation(key, shards_of)[block_of(target)]
    far = (block_of(target) + shards_of // 2) % shards_of
    return jnp.where((block_of(source) == near) | (block_of(source) == far), factor * result, result)


def block_scale(key, extent, cuts, smallest, top_value):
    def one(axis_at, blocks):
        heights = jax.random.uniform(jax.random.fold_in(jax.random.fold_in(key, 6), axis_at), (blocks,), jnp.float32, smallest / len(cuts), top_value / len(cuts))
        return jnp.repeat(jnp.exp(heights), extent[axis_at] // blocks).reshape((-1,) + (1,) * (len(extent) - axis_at - 1))

    level = one(*cuts[0])
    for cut in cuts[1:]:
        level = level * one(*cut)
    return level


def noise(rng, shape, spread, reach, shards=(), held_as=jnp.bfloat16):
    entries = jax.random.normal(rng, shape, jnp.float32) * spread
    if len(shards) > 0:
        entries = block_scale(rng, shape, shards, -0.22, 0.18) * entries
    return jnp.clip(entries, min=-reach, max=reach).astype(held_as)


def heavy_noise(stream_key, dims, spread, limit, shards, heavy, kind=jnp.bfloat16):
    drawn = spread * jax.random.normal(stream_key, dims, jnp.float32)
    if shards:
        drawn = drawn * block_scale(stream_key, dims, shards, -0.22, 0.18)
    return jnp.clip(raised(drawn, jax.random.fold_in(stream_key, 3), *heavy), -limit, limit).astype(kind)


def setup_inputs(seed: int = 0) -> dict:
    streams_of = jax.random.split(jax.random.key(seed), 7)
    amplitudes = noise(streams_of[0], (OO, CD), 1.0, 6.0, ((0, 16), (1, 16)))
    integrals = heavy_noise(streams_of[1], (CD, AB), CD ** -0.5, 0.01953125, ((0, 16), (1, 16)), (0, 1, 16, 2.0))
    pair_first = touch_ends(jax.random.randint(streams_of[2], (AB,), 0, NVIR), jax.random.fold_in(streams_of[2], 1), 0, NVIR - 1).astype(jnp.int32)
    pair_second = touch_ends(jax.random.randint(streams_of[3], (AB,), 0, NVIR), jax.random.fold_in(streams_of[3], 1), 0, NVIR - 1).astype(jnp.int32)
    occ_energy = jnp.clip(jax.random.uniform(streams_of[4], (NOCC,), jnp.float32, -1.0, -0.5), -1.0, -0.5)
    vir_energy = jnp.clip(jax.random.uniform(streams_of[5], (NVIR,), jnp.float32, 0.25, 1.0), 0.25, 1.0)
    return dict(amplitudes=amplitudes, integrals=integrals, pair_first=pair_first, pair_second=pair_second, occ_energy=occ_energy, vir_energy=vir_energy)


def reference(amplitudes, integrals, pair_first, pair_second, occ_energy, vir_energy):
    ladder = jnp.dot(amplitudes, integrals, preferred_element_type=jnp.float32)
    pair_rows = jnp.arange(amplitudes.shape[0], dtype=jnp.int32)
    first_occ = occ_energy[pair_rows // NOCC]
    second_occ = occ_energy[pair_rows % NOCC]
    first_vir = vir_energy[pair_first]
    second_vir = vir_energy[pair_second]
    denominator = first_occ[:, None] + second_occ[:, None] - first_vir[None, :] - second_vir[None, :]
    return (ladder / denominator).astype(jnp.bfloat16)
```

```python
import functools

import jax
import jax.numpy as jnp
from jax import lax
from jax.experimental import pallas as pl
from jax.experimental.pallas import tpu as pltpu
from jax.sharding import PartitionSpec as P

YS, ZS = 4, 8
STEP = {"x": (1, 0), "U": (0, 1), "D": (0, -1)}
SLICES = ((64, (0, 0, 0, 1, 1, 2, 4), "DUxxDxD", "xUDUDUU"),)
DEPTH = 2048
GROUPS = (((0, 4), (4, 7), (7, 8)),)
ORDER = (
    ("s00", ()), ("s01", ()), ("s02", ()), ("s03", ("own",)), ("s04", ("s00",)), ("s05", ("s01",)),
    ("m00", ()), ("s06", ("m00",)), ("m01", ()), ("m02", ("m01",)),
)


def places(sources, ways):
    at = [(0, 0)]
    for source, way in zip(sources, ways):
        dx, dy = at[source]
        at.append((dx ^ STEP[way][0], (dy + STEP[way][1]) % YS))
    return at


def row_perm(ways):
    return [
        ((x * YS + y) * 2 + c, ((x ^ STEP[w][0]) * YS + (y + STEP[w][1]) % YS) * 2 + c)
        for x in range(2)
        for y in range(YS)
        for c, w in enumerate(ways)
    ]


PARTNER = [(r, r ^ 1) for r in range(4 * YS)]


def swap_perm(flip):
    pairs = []
    for xy in range(2 * YS):
        for c in range(2):
            for z in range(ZS):
                for h in range(2):
                    pairs.append((((xy * 2 + c) * ZS + z) * 2 + h, ((xy * 2 + (h ^ flip)) * ZS + z) * 2 + c))
    return pairs


def lookup(indices, table):
    places = jnp.arange(table.shape[0], dtype=jnp.int32)
    return jnp.sum(jnp.where(indices[:, None] == places[None, :], table[None, :], 0.0), axis=1)


def turn_kernel(rows, out):
    out[...] = rows[...].T


def turned(amplitudes):
    rows, depth = amplitudes.shape
    return pl.pallas_call(
        turn_kernel,
        grid=(depth // DEPTH,),
        in_specs=[pl.BlockSpec((rows, DEPTH), lambda k: (0, k))],
        out_specs=pl.BlockSpec((DEPTH, rows), lambda k: (k, 0)),
        out_shape=jax.ShapeDtypeStruct((depth, rows), amplitudes.dtype),
        cost_estimate=pl.CostEstimate(flops=0, bytes_accessed=0, transcendentals=0),
    )(amplitudes)


def accumulate(total, blocks, amplitudes):
    step = pl.program_id(0)
    stacked = jnp.concatenate([block[...] for block in blocks], axis=0)
    for half, rows in enumerate(amplitudes):
        count = rows.shape[1]
        columns = slice(half * count, (half + 1) * count)
        part = jnp.dot(stacked, rows[...], preferred_element_type=jnp.float32)

        @pl.when(step == 0)
        def _():
            total[:, columns] = part

        @pl.when(step > 0)
        def _():
            total[:, columns] += part


def product_kernel(*refs):
    *blocks, own, other, total = refs
    accumulate(total, blocks, (own, other))


def finish_kernel(counts, spots, *refs):
    last = counts[-1]
    blocks, (own, other) = refs[:last], refs[last : last + 2]
    earlier, out, total = refs[last + 2 : -2], refs[-2], refs[-1]
    accumulate(total, blocks, (own, other))

    @pl.when(pl.program_id(0) == pl.num_programs(0) - 1)
    def _():
        row = lax.axis_index("row")
        x, y, core = row // (2 * YS), row // 2 % YS, row % 2
        n = out.shape[1]
        i = 0
        for count, sums in zip(counts, (*earlier, total)):
            for j in range(count):
                (x0, y0), (x1, y1) = spots[0][i], spots[1][i]
                from_x = jnp.where(core == 0, x ^ x0, x ^ x1)
                from_y = jnp.where(core == 0, (y + YS - y0) % YS, (y + YS - y1) % YS)
                out[from_x * YS + from_y] = sums[j * n : (j + 1) * n, :]
                i += 1


def multiply(kernel, blocks, own, other, earlier, out_shape, scratch):
    n, depth = blocks[0].shape
    rows = own.shape[1]
    whole = lambda shape: pl.BlockSpec(shape, lambda k: (0,) * len(shape))
    return pl.pallas_call(
        kernel,
        grid=(depth // DEPTH,),
        in_specs=[pl.BlockSpec((n, DEPTH), lambda k: (0, k))] * len(blocks)
        + [pl.BlockSpec((DEPTH, rows), lambda k: (k, 0))] * 2
        + [whole(sums.shape) for sums in earlier],
        out_specs=whole(out_shape),
        out_shape=jax.ShapeDtypeStruct(out_shape, jnp.float32),
        scratch_shapes=scratch,
        compiler_params=pltpu.CompilerParams(vmem_limit_bytes=16 * 1024 * 1024),
        cost_estimate=pl.CostEstimate(flops=0, bytes_accessed=0, transcendentals=0),
    )(*blocks, own, other, *earlier)


def sums_of(blocks, own, other):
    n, width = blocks[0].shape[0], 2 * own.shape[1]
    return multiply(product_kernel, blocks, own, other, (), (len(blocks) * n, width), ())


def last_sums(blocks, own, other, earlier, spots, groups):
    n, width = blocks[0].shape[0], 2 * own.shape[1]
    counts = tuple(b - a for a, b in groups)
    kernel = functools.partial(finish_kernel, counts, spots)
    scratch = [pltpu.VMEM((len(blocks) * n, width), jnp.float32)]
    return multiply(kernel, blocks, own, other, earlier, (8, n, width), scratch)


def after(value, *others):
    return lax.optimization_barrier((value, *others))[0]


def partials(rows, amplitudes):
    done = {"other": turned(lax.ppermute(amplitudes, "row", PARTNER)), "own": turned(amplitudes)}
    held, earlier, start = [], [], 0
    for n, *_ in SLICES:
        held.append([lax.slice_in_dim(rows, start, start + n, axis=0)])
        earlier.append([])
        start += n
    for name, needs in ORDER:
        s, i = int(name[1]), int(name[2])
        n, sources, first, second = SLICES[s]
        if name[0] == "s":
            block = after(held[s][sources[i]], *(done[need] for need in needs))
            done[name] = lax.ppermute(block, "row", row_perm((first[i], second[i])))
            held[s].append(done[name])
            continue
        a, b = GROUPS[s][i]
        blocks = held[s][a:b]
        blocks[0] = after(blocks[0], *(done[need] for need in needs))
        if b < 8:
            done[name] = sums_of(blocks, done["own"], done["other"])
            earlier[s].append(done[name])
        else:
            spots = (places(sources, first), places(sources, second))
            done[name] = last_sums(blocks, done["own"], done["other"], earlier[s], spots, GROUPS[s])
            yield done[name]


def on_device(amplitudes, integrals, pair_first, pair_second, occ_energy, vir_energy):
    local_rows = amplitudes.shape[0]
    row, col = lax.axis_index("row"), lax.axis_index("col")
    core, h = row % 2, col % 2
    same = h == core
    along_z = [[z * 2 + b for z in range(ZS)] for b in range(2)]
    done = []
    for sums in partials(integrals.T, amplitudes):
        if done:
            sums = after(sums, shares)
        shares = lax.all_to_all(sums, "col", split_axis=0, concat_axis=0, tiled=True, axis_index_groups=along_z)
        mine = jnp.sum(shares, axis=0)
        own, theirs = mine[:, :local_rows], mine[:, local_rows:]
        a = lax.ppermute(jnp.where(same, own, theirs), ("row", "col"), swap_perm(0))
        b = lax.ppermute(jnp.where(same, theirs, own), ("row", "col"), swap_perm(1))
        done.append(a + b)
    ladder = jnp.concatenate(done, axis=0)

    nocc_count = occ_energy.shape[0]
    pair_rows = row * local_rows + jnp.arange(local_rows, dtype=jnp.int32)
    first_occ = lookup(pair_rows // nocc_count, occ_energy)
    second_occ = lookup(pair_rows % nocc_count, occ_energy)
    first_vir = lookup(pair_first, vir_energy)
    second_vir = lookup(pair_second, vir_energy)
    denominator = (
        first_occ[None, :] + second_occ[None, :] - first_vir[:, None] - second_vir[:, None]
    )
    return (ladder / denominator).astype(jnp.bfloat16).T


def solution(mesh):
    placed = (P("row", "col"), P("col", "row"), P("col"), P("col"), P(), P())
    return jax.shard_map(
        on_device, mesh=mesh, in_specs=placed, out_specs=P("row", "col"), check_vma=False
    )
```

```python
import functools

import jax
import jax.numpy as jnp
from jax import lax
from jax.experimental import pallas as pl
from jax.experimental.pallas import tpu as pltpu
from jax.sharding import PartitionSpec as P

YS, ZS = 4, 8
STEP = {"x": (1, 0), "U": (0, 1), "D": (0, -1)}
SLICES = ((64, (0, 0, 0, 1, 1, 2, 4), "DUxxDxD", "xUDUDUU"),)
UNITS = 32767.0
SMALLEST = 2.0**-126
DEPTH = 2048
GROUPS = (((0, 4), (4, 7), (7, 8)),)
ORDER = (
    ("s00", ()), ("s01", ()), ("s02", ()), ("s03", ("own",)), ("s04", ("s00",)), ("s05", ("s01",)),
    ("m00", ()), ("s06", ("m00",)), ("m01", ()), ("m02", ("m01",)),
)


def places(sources, ways):
    at = [(0, 0)]
    for source, way in zip(sources, ways):
        dx, dy = at[source]
        at.append((dx ^ STEP[way][0], (dy + STEP[way][1]) % YS))
    return at


def row_perm(ways):
    return [
        ((x * YS + y) * 2 + c, ((x ^ STEP[w][0]) * YS + (y + STEP[w][1]) % YS) * 2 + c)
        for x in range(2)
        for y in range(YS)
        for c, w in enumerate(ways)
    ]


PARTNER = [(r, r ^ 1) for r in range(4 * YS)]


def swap_perm(flip):
    pairs = []
    for xy in range(2 * YS):
        for c in range(2):
            for z in range(ZS):
                for h in range(2):
                    pairs.append((((xy * 2 + c) * ZS + z) * 2 + h, ((xy * 2 + (h ^ flip)) * ZS + z) * 2 + c))
    return pairs


def lookup(indices, table):
    places = jnp.arange(table.shape[0], dtype=jnp.int32)
    return jnp.sum(jnp.where(indices[:, None] == places[None, :], table[None, :], 0.0), axis=1)


def turn_kernel(rows, out):
    out[...] = rows[...].T


def turned(amplitudes):
    rows, depth = amplitudes.shape
    return pl.pallas_call(
        turn_kernel,
        grid=(depth // DEPTH,),
        in_specs=[pl.BlockSpec((rows, DEPTH), lambda k: (0, k))],
        out_specs=pl.BlockSpec((DEPTH, rows), lambda k: (k, 0)),
        out_shape=jax.ShapeDtypeStruct((depth, rows), amplitudes.dtype),
        cost_estimate=pl.CostEstimate(flops=0, bytes_accessed=0, transcendentals=0),
    )(amplitudes)


def accumulate(total, blocks, amplitudes):
    step = pl.program_id(0)
    stacked = jnp.concatenate([block[...] for block in blocks], axis=0)
    for half, rows in enumerate(amplitudes):
        count = rows.shape[1]
        columns = slice(half * count, (half + 1) * count)
        part = jnp.dot(stacked, rows[...], preferred_element_type=jnp.float32)

        @pl.when(step == 0)
        def _():
            total[:, columns] = part

        @pl.when(step > 0)
        def _():
            total[:, columns] += part


def product_kernel(*refs):
    *blocks, own, other, total = refs
    accumulate(total, blocks, (own, other))


def coded(sums):
    largest = jnp.maximum(jnp.max(jnp.abs(sums), axis=1, keepdims=True), SMALLEST)
    power = jnp.clip(jnp.floor(jnp.log2(largest)) + 1.0, -126.0, 126.0)
    scaled = sums * jnp.exp2(-power)
    part = jnp.ceil(largest * jnp.exp2(-power) * 256.0)
    whole = jnp.round(scaled * (256.0 * UNITS / part))
    place = lax.broadcasted_iota(jnp.int32, (sums.shape[0], 128), 1)
    note = jnp.where(place == 0, power, part)
    return jnp.concatenate([whole, note], axis=1).astype(jnp.int32).astype(jnp.int16)


def decoded(shares):
    width = shares.shape[-1] - 128
    whole = shares[..., :width].astype(jnp.float32)
    power = shares[..., width : width + 1].astype(jnp.float32)
    part = shares[..., width + 1 : width + 2].astype(jnp.float32)
    return whole * (part * (1.0 / (256.0 * UNITS))) * jnp.exp2(power)


def finish_kernel(counts, spots, *refs):
    last = counts[-1]
    blocks, (own, other) = refs[:last], refs[last : last + 2]
    earlier, out, total = refs[last + 2 : -2], refs[-2], refs[-1]
    accumulate(total, blocks, (own, other))

    @pl.when(pl.program_id(0) == pl.num_programs(0) - 1)
    def _():
        row = lax.axis_index("row")
        x, y, core = row // (2 * YS), row // 2 % YS, row % 2
        n = out.shape[1]
        i = 0
        for count, sums in zip(counts, (*earlier, total)):
            for j in range(count):
                (x0, y0), (x1, y1) = spots[0][i], spots[1][i]
                from_x = jnp.where(core == 0, x ^ x0, x ^ x1)
                from_y = jnp.where(core == 0, (y + YS - y0) % YS, (y + YS - y1) % YS)
                out[from_x * YS + from_y] = coded(sums[j * n : (j + 1) * n, :])
                i += 1


def multiply(kernel, blocks, own, other, earlier, out_shape, scratch, kind=jnp.float32):
    n, depth = blocks[0].shape
    rows = own.shape[1]
    whole = lambda shape: pl.BlockSpec(shape, lambda k: (0,) * len(shape))
    return pl.pallas_call(
        kernel,
        grid=(depth // DEPTH,),
        in_specs=[pl.BlockSpec((n, DEPTH), lambda k: (0, k))] * len(blocks)
        + [pl.BlockSpec((DEPTH, rows), lambda k: (k, 0))] * 2
        + [whole(sums.shape) for sums in earlier],
        out_specs=whole(out_shape),
        out_shape=jax.ShapeDtypeStruct(out_shape, kind),
        scratch_shapes=scratch,
        compiler_params=pltpu.CompilerParams(vmem_limit_bytes=16 * 1024 * 1024),
        cost_estimate=pl.CostEstimate(flops=0, bytes_accessed=0, transcendentals=0),
    )(*blocks, own, other, *earlier)


def sums_of(blocks, own, other):
    n, width = blocks[0].shape[0], 2 * own.shape[1]
    return multiply(product_kernel, blocks, own, other, (), (len(blocks) * n, width), ())


def last_sums(blocks, own, other, earlier, spots, groups):
    n, width = blocks[0].shape[0], 2 * own.shape[1]
    counts = tuple(b - a for a, b in groups)
    kernel = functools.partial(finish_kernel, counts, spots)
    scratch = [pltpu.VMEM((len(blocks) * n, width), jnp.float32)]
    return multiply(kernel, blocks, own, other, earlier, (8, n, width + 128), scratch, jnp.int16)


def after(value, *others):
    return lax.optimization_barrier((value, *others))[0]


def partials(rows, amplitudes):
    done = {"other": turned(lax.ppermute(amplitudes, "row", PARTNER)), "own": turned(amplitudes)}
    held, earlier, start = [], [], 0
    for n, *_ in SLICES:
        held.append([lax.slice_in_dim(rows, start, start + n, axis=0)])
        earlier.append([])
        start += n
    for name, needs in ORDER:
        s, i = int(name[1]), int(name[2])
        n, sources, first, second = SLICES[s]
        if name[0] == "s":
            block = after(held[s][sources[i]], *(done[need] for need in needs))
            done[name] = lax.ppermute(block, "row", row_perm((first[i], second[i])))
            held[s].append(done[name])
            continue
        a, b = GROUPS[s][i]
        blocks = held[s][a:b]
        blocks[0] = after(blocks[0], *(done[need] for need in needs))
        if b < 8:
            done[name] = sums_of(blocks, done["own"], done["other"])
            earlier[s].append(done[name])
        else:
            spots = (places(sources, first), places(sources, second))
            done[name] = last_sums(blocks, done["own"], done["other"], earlier[s], spots, GROUPS[s])
            yield done[name]


def on_device(amplitudes, integrals, pair_first, pair_second, occ_energy, vir_energy):
    local_rows = amplitudes.shape[0]
    row, col = lax.axis_index("row"), lax.axis_index("col")
    core, h = row % 2, col % 2
    same = h == core
    along_z = [[z * 2 + b for z in range(ZS)] for b in range(2)]
    done = []
    for sums in partials(integrals.T, amplitudes):
        if done:
            sums = after(sums, shares)
        shares = lax.all_to_all(sums, "col", split_axis=0, concat_axis=0, tiled=True, axis_index_groups=along_z)
        mine = jnp.sum(decoded(shares), axis=0)
        own, theirs = mine[:, :local_rows], mine[:, local_rows:]
        a = lax.ppermute(jnp.where(same, own, theirs), ("row", "col"), swap_perm(0))
        b = lax.ppermute(jnp.where(same, theirs, own), ("row", "col"), swap_perm(1))
        done.append(a + b)
    ladder = jnp.concatenate(done, axis=0)

    nocc_count = occ_energy.shape[0]
    pair_rows = row * local_rows + jnp.arange(local_rows, dtype=jnp.int32)
    first_occ = lookup(pair_rows // nocc_count, occ_energy)
    second_occ = lookup(pair_rows % nocc_count, occ_energy)
    first_vir = lookup(pair_first, vir_energy)
    second_vir = lookup(pair_second, vir_energy)
    denominator = (
        first_occ[None, :] + second_occ[None, :] - first_vir[:, None] - second_vir[:, None]
    )
    return (ladder / denominator).astype(jnp.bfloat16).T


def solution(mesh):
    placed = (P("row", "col"), P("col", "row"), P("col"), P("col"), P(), P())
    return jax.shard_map(
        on_device, mesh=mesh, in_specs=placed, out_specs=P("row", "col"), check_vma=False
    )
```

```python
import functools

import jax
import jax.numpy as jnp
from jax import lax
from jax.experimental import pallas as pl
from jax.experimental.pallas import tpu as pltpu
from jax.sharding import PartitionSpec as P

YS, ZS = 4, 8
STEP = {"x": (1, 0), "U": (0, 1), "D": (0, -1)}
SLICES = ((64, (0, 0, 0, 1, 1, 2, 4), "DUxxDxD", "xUDUDUU"),)
UNITS = 32767.0
SMALLEST = 2.0**-126
LAST_DEPTH = 2048
DEPTH = 2048
GROUPS = (((0, 4), (4, 6), (6, 8)),)
ORDER = (
    ("s00", ()), ("s01", ()), ("s02", ()), ("s03", ("own",)), ("s04", ("s00",)), ("s05", ("s01",)),
    ("m00", ()), ("s06", ("m00",)), ("m01", ()), ("m02", ("m01",)),
)


def places(sources, ways):
    at = [(0, 0)]
    for source, way in zip(sources, ways):
        dx, dy = at[source]
        at.append((dx ^ STEP[way][0], (dy + STEP[way][1]) % YS))
    return at


def row_perm(ways):
    return [
        ((x * YS + y) * 2 + c, ((x ^ STEP[w][0]) * YS + (y + STEP[w][1]) % YS) * 2 + c)
        for x in range(2)
        for y in range(YS)
        for c, w in enumerate(ways)
    ]


PARTNER = [(r, r ^ 1) for r in range(4 * YS)]


def swap_perm(flip):
    pairs = []
    for xy in range(2 * YS):
        for c in range(2):
            for z in range(ZS):
                for h in range(2):
                    pairs.append((((xy * 2 + c) * ZS + z) * 2 + h, ((xy * 2 + (h ^ flip)) * ZS + z) * 2 + c))
    return pairs


def lookup(indices, table):
    places = jnp.arange(table.shape[0], dtype=jnp.int32)
    return jnp.sum(jnp.where(indices[:, None] == places[None, :], table[None, :], 0.0), axis=1)


def turn_kernel(rows, out):
    out[...] = rows[...].T


def turned(amplitudes):
    rows, depth = amplitudes.shape
    return pl.pallas_call(
        turn_kernel,
        grid=(depth // DEPTH,),
        in_specs=[pl.BlockSpec((rows, DEPTH), lambda k: (0, k))],
        out_specs=pl.BlockSpec((DEPTH, rows), lambda k: (k, 0)),
        out_shape=jax.ShapeDtypeStruct((depth, rows), amplitudes.dtype),
        compiler_params=pltpu.CompilerParams(vmem_limit_bytes=8 * 1024 * 1024),
        cost_estimate=pl.CostEstimate(flops=0, bytes_accessed=0, transcendentals=0),
    )(amplitudes)


def accumulate(total, blocks, amplitudes):
    step = pl.program_id(0)
    stacked = jnp.concatenate([block[...] for block in blocks], axis=0)
    for half, rows in enumerate(amplitudes):
        count = rows.shape[1]
        columns = slice(half * count, (half + 1) * count)
        part = jnp.dot(stacked, rows[...], preferred_element_type=jnp.float32)

        @pl.when(step == 0)
        def _():
            total[:, columns] = part

        @pl.when(step > 0)
        def _():
            total[:, columns] += part


def product_kernel(*refs):
    *blocks, own, other, total = refs
    accumulate(total, blocks, (own, other))


def coded(sums):
    largest = jnp.maximum(jnp.max(jnp.abs(sums), axis=1, keepdims=True), SMALLEST)
    power = jnp.clip(jnp.floor(jnp.log2(largest)) + 1.0, -126.0, 126.0)
    scale = jnp.exp2(-power)
    part = jnp.ceil(largest * scale * 256.0)
    whole = jnp.round(sums * scale * (256.0 * UNITS / part))
    place = lax.broadcasted_iota(jnp.int32, (16, 128), 1)
    note = jnp.zeros((16, 128), jnp.float32)
    pieces = []
    for g in range(sums.shape[0] // 16):
        these = slice(g * 16, (g + 1) * 16)
        note = jnp.where(place == 2 * g, power[these], jnp.where(place == 2 * g + 1, part[these], note))
        pieces.append(whole[these])
    return jnp.concatenate([*pieces, note], axis=1).astype(jnp.int32).astype(jnp.int16)


def coded_shape(rows, width):
    return (16, rows // 16 * width + 128)


def decoded(share, width):
    count = share.shape[1] // width
    rows = []
    for g in range(count):
        note = share[:, count * width :].astype(jnp.float32)
        power, part = note[:, 2 * g : 2 * g + 1], note[:, 2 * g + 1 : 2 * g + 2]
        scale = part * (1.0 / (256.0 * UNITS)) * jnp.exp2(power)
        rows.append(share[:, g * width : (g + 1) * width].astype(jnp.float32) * scale)
    return jnp.concatenate(rows, axis=0)


def finish_kernel(counts, spots, *refs):
    last = counts[-1]
    blocks, (own, other), earlier = refs[:last], refs[last : last + 2], refs[last + 2 : -6]
    kept, up, down, far, total, ordered = refs[-6:]
    accumulate(total, blocks, (own, other))

    @pl.when(pl.program_id(0) == pl.num_programs(0) - 1)
    def _():
        row, z = lax.axis_index("row"), lax.axis_index("col") // 2
        x, y, core = row // (2 * YS), row // 2 % YS, row % 2
        n = ordered.shape[1]
        i = 0
        for count, sums in zip(counts, (*earlier, total)):
            for j in range(count):
                (x0, y0), (x1, y1) = spots[0][i], spots[1][i]
                from_x = jnp.where(core == 0, x ^ x0, x ^ x1)
                from_y = jnp.where(core == 0, (y + YS - y0) % YS, (y + YS - y1) % YS)
                ordered[(from_x * YS + from_y + ZS - z) % ZS] = sums[j * n : (j + 1) * n, :]
                i += 1
        for place, step in enumerate((0, 2, 6)):
            kept[place] = ordered[step]
        up[0], up[1] = coded(ordered[1]), coded(ordered[3])
        down[0], down[1] = coded(ordered[7]), coded(ordered[5])
        far[...] = coded(ordered[4])


def pass_kernel(kept, from_below, from_above, from_far, up, down):
    width = kept.shape[2]
    even = (lax.axis_index("col") // 2) % 2 == 0
    far = decoded(from_far[...], width)
    up[...] = coded(kept[1] + decoded(from_below[1], width) + jnp.where(even, far, 0.0))
    down[...] = coded(kept[2] + decoded(from_above[1], width) + jnp.where(even, 0.0, far))


def along_z(sums, even, odd):
    pairs = [(a * 2 + b, (a + (odd if a % 2 else even)) % ZS * 2 + b) for a in range(ZS) for b in range(2)]
    return lax.ppermute(sums, "col", pairs)


def sum_along_z(kept, up, down, far):
    _, n, width = kept.shape
    from_far = along_z(far, 2, -2)
    from_below, from_above = along_z(up, 1, 1), along_z(down, -1, -1)
    shape = jax.ShapeDtypeStruct(coded_shape(n, width), jnp.int16)
    up, down = pl.pallas_call(
        pass_kernel,
        out_shape=[shape, shape],
        compiler_params=pltpu.CompilerParams(vmem_limit_bytes=12 * 1024 * 1024),
        cost_estimate=pl.CostEstimate(flops=0, bytes_accessed=0, transcendentals=0),
    )(kept, from_below, from_above, from_far)
    near = (from_below[0], from_above[0], along_z(up, 2, 2), along_z(down, -2, -2))
    return kept[0] + sum(decoded(share, width) for share in near)


def multiply(kernel, blocks, own, other, earlier, outs, scratch, step=DEPTH, room=16):
    n, depth = blocks[0].shape
    rows = own.shape[1]
    whole = lambda shape: pl.BlockSpec(shape, lambda k: (0,) * len(shape))
    return pl.pallas_call(
        kernel,
        grid=(depth // step,),
        in_specs=[pl.BlockSpec((n, step), lambda k: (0, k))] * len(blocks)
        + [pl.BlockSpec((step, rows), lambda k: (k, 0))] * 2
        + [whole(sums.shape) for sums in earlier],
        out_specs=[whole(out.shape) for out in outs],
        out_shape=list(outs),
        scratch_shapes=scratch,
        compiler_params=pltpu.CompilerParams(vmem_limit_bytes=room * 1024 * 1024),
        cost_estimate=pl.CostEstimate(flops=0, bytes_accessed=0, transcendentals=0),
    )(*blocks, own, other, *earlier)


def sums_of(blocks, own, other):
    n, width = blocks[0].shape[0], 2 * own.shape[1]
    out = jax.ShapeDtypeStruct((len(blocks) * n, width), jnp.float32)
    return multiply(product_kernel, blocks, own, other, (), (out,), ())[0]


def last_sums(blocks, own, other, earlier, spots, groups):
    n, width = blocks[0].shape[0], 2 * own.shape[1]
    counts = tuple(b - a for a, b in groups)
    kernel = functools.partial(finish_kernel, counts, spots)
    scratch = [pltpu.VMEM((len(blocks) * n, width), jnp.float32), pltpu.VMEM((8, n, width), jnp.float32)]
    one = coded_shape(n, width)
    pair = jax.ShapeDtypeStruct((2, *one), jnp.int16)
    outs = (jax.ShapeDtypeStruct((3, n, width), jnp.float32), pair, pair, jax.ShapeDtypeStruct(one, jnp.int16))
    return multiply(kernel, blocks, own, other, earlier, outs, scratch, LAST_DEPTH, 18)


def after(value, *others):
    return lax.optimization_barrier((value, *others))[0]


def partials(rows, amplitudes):
    done = {"other": turned(lax.ppermute(amplitudes, "row", PARTNER)), "own": turned(amplitudes)}
    held, earlier, start = [], [], 0
    for n, *_ in SLICES:
        held.append([lax.slice_in_dim(rows, start, start + n, axis=0)])
        earlier.append([])
        start += n
    for name, needs in ORDER:
        s, i = int(name[1]), int(name[2])
        n, sources, first, second = SLICES[s]
        if name[0] == "s":
            block = after(held[s][sources[i]], *(done[need] for need in needs))
            done[name] = lax.ppermute(block, "row", row_perm((first[i], second[i])))
            held[s].append(done[name])
            continue
        a, b = GROUPS[s][i]
        blocks = held[s][a:b]
        blocks[0] = after(blocks[0], *(done[need] for need in needs))
        if b < 8:
            done[name] = sums_of(blocks, done["own"], done["other"])
            earlier[s].append(done[name])
        else:
            spots = (places(sources, first), places(sources, second))
            done[name] = last_sums(blocks, done["own"], done["other"], earlier[s], spots, GROUPS[s])
            return done[name]


def on_device(amplitudes, integrals, pair_first, pair_second, occ_energy, vir_energy):
    local_rows = amplitudes.shape[0]
    row, col = lax.axis_index("row"), lax.axis_index("col")
    core, h = row % 2, col % 2
    same = h == core
    mine = sum_along_z(*partials(integrals.T, amplitudes))
    own, theirs = mine[:, :local_rows], mine[:, local_rows:]
    ladder = lax.ppermute(jnp.where(same, own, theirs), ("row", "col"), swap_perm(0)) + lax.ppermute(
        jnp.where(same, theirs, own), ("row", "col"), swap_perm(1)
    )

    nocc_count = occ_energy.shape[0]
    pair_rows = row * local_rows + jnp.arange(local_rows, dtype=jnp.int32)
    first_occ = lookup(pair_rows // nocc_count, occ_energy)
    second_occ = lookup(pair_rows % nocc_count, occ_energy)
    first_vir = lookup(pair_first, vir_energy)
    second_vir = lookup(pair_second, vir_energy)
    denominator = (
        first_occ[None, :] + second_occ[None, :] - first_vir[:, None] - second_vir[:, None]
    )
    return (ladder / denominator).astype(jnp.bfloat16).T


def solution(mesh):
    placed = (P("row", "col"), P("col", "row"), P("col"), P("col"), P(), P())
    return jax.shard_map(
        on_device, mesh=mesh, in_specs=placed, out_specs=P("row", "col"), check_vma=False
    )
```

```python
import functools

import jax
import jax.numpy as jnp
from jax import lax
from jax.experimental import pallas as pl
from jax.experimental.pallas import tpu as pltpu
from jax.sharding import PartitionSpec as P

YS, ZS = 4, 8
STEP = {"x": (1, 0), "U": (0, 1), "D": (0, -1)}
SLICES = ((64, (0, 0, 0, 1, 1, 2, 4), "DUxxDxD", "xUDUDUU"),)
UNITS = 32767.0
SMALLEST = 2.0**-126
LAST_DEPTH = 5120
DEPTH = 2048
GROUPS = (((0, 4), (4, 6), (6, 8)),)
ORDER = (
    ("s00", ()), ("s01", ()), ("s02", ()), ("s03", ("own",)), ("s04", ("s00",)), ("s05", ("s01",)),
    ("m00", ()), ("s06", ("m00",)), ("m01", ()), ("m02", ("m01",)),
)


def places(sources, ways):
    at = [(0, 0)]
    for source, way in zip(sources, ways):
        dx, dy = at[source]
        at.append((dx ^ STEP[way][0], (dy + STEP[way][1]) % YS))
    return at


def row_perm(ways):
    return [
        ((x * YS + y) * 2 + c, ((x ^ STEP[w][0]) * YS + (y + STEP[w][1]) % YS) * 2 + c)
        for x in range(2)
        for y in range(YS)
        for c, w in enumerate(ways)
    ]


PARTNER = [(r, r ^ 1) for r in range(4 * YS)]


def swap_perm(flip):
    pairs = []
    for xy in range(2 * YS):
        for c in range(2):
            for z in range(ZS):
                for h in range(2):
                    pairs.append((((xy * 2 + c) * ZS + z) * 2 + h, ((xy * 2 + (h ^ flip)) * ZS + z) * 2 + c))
    return pairs


def lookup(indices, table):
    places = jnp.arange(table.shape[0], dtype=jnp.int32)
    return jnp.sum(jnp.where(indices[:, None] == places[None, :], table[None, :], 0.0), axis=1)


def turn_kernel(rows, out):
    out[...] = rows[...].T


def turned(amplitudes):
    rows, depth = amplitudes.shape
    return pl.pallas_call(
        turn_kernel,
        grid=(depth // DEPTH,),
        in_specs=[pl.BlockSpec((rows, DEPTH), lambda k: (0, k))],
        out_specs=pl.BlockSpec((DEPTH, rows), lambda k: (k, 0)),
        out_shape=jax.ShapeDtypeStruct((depth, rows), amplitudes.dtype),
        compiler_params=pltpu.CompilerParams(vmem_limit_bytes=8 * 1024 * 1024),
        cost_estimate=pl.CostEstimate(flops=0, bytes_accessed=0, transcendentals=0),
    )(amplitudes)


def accumulate(total, blocks, amplitudes):
    step = pl.program_id(0)
    stacked = jnp.concatenate([block[...] for block in blocks], axis=0)
    for half, rows in enumerate(amplitudes):
        count = rows.shape[1]
        columns = slice(half * count, (half + 1) * count)
        part = jnp.dot(stacked, rows[...], preferred_element_type=jnp.float32)

        @pl.when(step == 0)
        def _():
            total[:, columns] = part

        @pl.when(step > 0)
        def _():
            total[:, columns] += part


def product_kernel(*refs):
    *blocks, own, other, total = refs
    accumulate(total, blocks, (own, other))


def coded(sums):
    largest = jnp.maximum(jnp.max(jnp.abs(sums), axis=1, keepdims=True), SMALLEST)
    power = jnp.clip(jnp.floor(jnp.log2(largest)) + 1.0, -126.0, 126.0)
    scale = jnp.exp2(-power)
    part = jnp.ceil(largest * scale * 256.0)
    whole = jnp.round(sums * scale * (256.0 * UNITS / part))
    place = lax.broadcasted_iota(jnp.int32, (16, 128), 1)
    note = jnp.zeros((16, 128), jnp.float32)
    pieces = []
    for g in range(sums.shape[0] // 16):
        these = slice(g * 16, (g + 1) * 16)
        note = jnp.where(place == 2 * g, power[these], jnp.where(place == 2 * g + 1, part[these], note))
        pieces.append(whole[these])
    return jnp.concatenate([*pieces, note], axis=1).astype(jnp.int32).astype(jnp.int16)


def coded_shape(rows, width):
    return (16, rows // 16 * width + 128)


def decoded(share, width):
    count = share.shape[1] // width
    rows = []
    for g in range(count):
        note = share[:, count * width :].astype(jnp.float32)
        power, part = note[:, 2 * g : 2 * g + 1], note[:, 2 * g + 1 : 2 * g + 2]
        scale = part * (1.0 / (256.0 * UNITS)) * jnp.exp2(power)
        rows.append(share[:, g * width : (g + 1) * width].astype(jnp.float32) * scale)
    return jnp.concatenate(rows, axis=0)


def finish_kernel(counts, spots, *refs):
    last = counts[-1]
    blocks, (own, other), earlier = refs[:last], refs[last : last + 2], refs[last + 2 : -6]
    kept, up, down, far, total, ordered = refs[-6:]
    accumulate(total, blocks, (own, other))

    @pl.when(pl.program_id(0) == pl.num_programs(0) - 1)
    def _():
        row, z = lax.axis_index("row"), lax.axis_index("col") // 2
        x, y, core = row // (2 * YS), row // 2 % YS, row % 2
        n = ordered.shape[1]
        i = 0
        for count, sums in zip(counts, (*earlier, total)):
            for j in range(count):
                (x0, y0), (x1, y1) = spots[0][i], spots[1][i]
                from_x = jnp.where(core == 0, x ^ x0, x ^ x1)
                from_y = jnp.where(core == 0, (y + YS - y0) % YS, (y + YS - y1) % YS)
                ordered[(from_x * YS + from_y + ZS - z) % ZS] = sums[j * n : (j + 1) * n, :]
                i += 1
        for place, step in enumerate((0, 2, 6)):
            kept[place] = ordered[step]
        up[0], up[1] = coded(ordered[1]), coded(ordered[3])
        down[0], down[1] = coded(ordered[7]), coded(ordered[5])
        far[...] = coded(ordered[4])


def pass_kernel(kept, from_below, from_above, from_far, up, down):
    width = kept.shape[2]
    even = (lax.axis_index("col") // 2) % 2 == 0
    far = decoded(from_far[...], width)
    up[...] = coded(kept[1] + decoded(from_below[1], width) + jnp.where(even, far, 0.0))
    down[...] = coded(kept[2] + decoded(from_above[1], width) + jnp.where(even, 0.0, far))


def along_z(sums, even, odd):
    pairs = [(a * 2 + b, (a + (odd if a % 2 else even)) % ZS * 2 + b) for a in range(ZS) for b in range(2)]
    return lax.ppermute(sums, "col", pairs)


def sum_along_z(kept, up, down, far):
    _, n, width = kept.shape
    from_far = along_z(far, 2, -2)
    from_below, from_above = along_z(up, 1, 1), along_z(down, -1, -1)
    shape = jax.ShapeDtypeStruct(coded_shape(n, width), jnp.int16)
    up, down = pl.pallas_call(
        pass_kernel,
        out_shape=[shape, shape],
        compiler_params=pltpu.CompilerParams(vmem_limit_bytes=12 * 1024 * 1024),
        cost_estimate=pl.CostEstimate(flops=0, bytes_accessed=0, transcendentals=0),
    )(kept, from_below, from_above, from_far)
    near = (from_below[0], from_above[0], along_z(up, 2, 2), along_z(down, -2, -2))
    return kept[0] + sum(decoded(share, width) for share in near)


def multiply(kernel, blocks, own, other, earlier, outs, scratch, step=DEPTH, room=16):
    n, depth = blocks[0].shape
    rows = own.shape[1]
    whole = lambda shape: pl.BlockSpec(shape, lambda k: (0,) * len(shape))
    return pl.pallas_call(
        kernel,
        grid=(depth // step,),
        in_specs=[pl.BlockSpec((n, step), lambda k: (0, k))] * len(blocks)
        + [pl.BlockSpec((step, rows), lambda k: (k, 0))] * 2
        + [whole(sums.shape) for sums in earlier],
        out_specs=[whole(out.shape) for out in outs],
        out_shape=list(outs),
        scratch_shapes=scratch,
        compiler_params=pltpu.CompilerParams(vmem_limit_bytes=room * 1024 * 1024),
        cost_estimate=pl.CostEstimate(flops=0, bytes_accessed=0, transcendentals=0),
    )(*blocks, own, other, *earlier)


def sums_of(blocks, own, other):
    n, width = blocks[0].shape[0], 2 * own.shape[1]
    out = jax.ShapeDtypeStruct((len(blocks) * n, width), jnp.float32)
    return multiply(product_kernel, blocks, own, other, (), (out,), ())[0]


def last_sums(blocks, own, other, earlier, spots, groups):
    n, width = blocks[0].shape[0], 2 * own.shape[1]
    counts = tuple(b - a for a, b in groups)
    kernel = functools.partial(finish_kernel, counts, spots)
    scratch = [pltpu.VMEM((len(blocks) * n, width), jnp.float32), pltpu.VMEM((8, n, width), jnp.float32)]
    one = coded_shape(n, width)
    pair = jax.ShapeDtypeStruct((2, *one), jnp.int16)
    outs = (jax.ShapeDtypeStruct((3, n, width), jnp.float32), pair, pair, jax.ShapeDtypeStruct(one, jnp.int16))
    return multiply(kernel, blocks, own, other, earlier, outs, scratch, LAST_DEPTH, 28)


def after(value, *others):
    return lax.optimization_barrier((value, *others))[0]


def partials(rows, amplitudes):
    done = {"other": turned(lax.ppermute(amplitudes, "row", PARTNER)), "own": turned(amplitudes)}
    held, earlier, start = [], [], 0
    for n, *_ in SLICES:
        held.append([lax.slice_in_dim(rows, start, start + n, axis=0)])
        earlier.append([])
        start += n
    for name, needs in ORDER:
        s, i = int(name[1]), int(name[2])
        n, sources, first, second = SLICES[s]
        if name[0] == "s":
            block = after(held[s][sources[i]], *(done[need] for need in needs))
            done[name] = lax.ppermute(block, "row", row_perm((first[i], second[i])))
            held[s].append(done[name])
            continue
        a, b = GROUPS[s][i]
        blocks = held[s][a:b]
        blocks[0] = after(blocks[0], *(done[need] for need in needs))
        if b < 8:
            done[name] = sums_of(blocks, done["own"], done["other"])
            earlier[s].append(done[name])
        else:
            spots = (places(sources, first), places(sources, second))
            done[name] = last_sums(blocks, done["own"], done["other"], earlier[s], spots, GROUPS[s])
            return done[name]


def on_device(amplitudes, integrals, pair_first, pair_second, occ_energy, vir_energy):
    local_rows = amplitudes.shape[0]
    row, col = lax.axis_index("row"), lax.axis_index("col")
    core, h = row % 2, col % 2
    same = h == core
    mine = sum_along_z(*partials(integrals.T, amplitudes))
    own, theirs = mine[:, :local_rows], mine[:, local_rows:]
    ladder = lax.ppermute(jnp.where(same, own, theirs), ("row", "col"), swap_perm(0)) + lax.ppermute(
        jnp.where(same, theirs, own), ("row", "col"), swap_perm(1)
    )

    nocc_count = occ_energy.shape[0]
    pair_rows = row * local_rows + jnp.arange(local_rows, dtype=jnp.int32)
    first_occ = lookup(pair_rows // nocc_count, occ_energy)
    second_occ = lookup(pair_rows % nocc_count, occ_energy)
    first_vir = lookup(pair_first, vir_energy)
    second_vir = lookup(pair_second, vir_energy)
    denominator = (
        first_occ[None, :] + second_occ[None, :] - first_vir[:, None] - second_vir[:, None]
    )
    return (ladder / denominator).astype(jnp.bfloat16).T


def solution(mesh):
    placed = (P("row", "col"), P("col", "row"), P("col"), P("col"), P(), P())
    return jax.shard_map(
        on_device, mesh=mesh, in_specs=placed, out_specs=P("row", "col"), check_vma=False
    )
```

```python
import functools

import jax
import jax.numpy as jnp
from jax import lax
from jax.experimental import pallas as pl
from jax.experimental.pallas import tpu as pltpu
from jax.sharding import PartitionSpec as P

YS, ZS = 4, 8
STEP = {"x": (1, 0), "U": (0, 1), "D": (0, -1)}
SLICES = ((64, (0, 0, 0, 1, 1, 2, 4), "DUxxDxD", "xUDUDUU"),)
UNITS = 32767.0
SMALLEST = 2.0**-126
LAST_DEPTH = 5120
DEPTH = 2048
GROUPS = (((0, 4), (4, 6), (6, 8)),)
ORDER = (
    ("s00", ()), ("s01", ()), ("s02", ()), ("s03", ("own",)), ("s04", ("s00",)), ("s05", ("s01",)),
    ("m00", ()), ("s06", ("m00",)), ("m01", ()), ("m02", ("m01",)),
)


def places(sources, ways):
    at = [(0, 0)]
    for source, way in zip(sources, ways):
        dx, dy = at[source]
        at.append((dx ^ STEP[way][0], (dy + STEP[way][1]) % YS))
    return at


def row_perm(ways):
    return [
        ((x * YS + y) * 2 + c, ((x ^ STEP[w][0]) * YS + (y + STEP[w][1]) % YS) * 2 + c)
        for x in range(2)
        for y in range(YS)
        for c, w in enumerate(ways)
    ]


PARTNER = [(r, r ^ 1) for r in range(4 * YS)]


def swap_perm(flip):
    pairs = []
    for xy in range(2 * YS):
        for c in range(2):
            for z in range(ZS):
                for h in range(2):
                    pairs.append((((xy * 2 + c) * ZS + z) * 2 + h, ((xy * 2 + (h ^ flip)) * ZS + z) * 2 + c))
    return pairs


def lookup(indices, table):
    places = jnp.arange(table.shape[0], dtype=jnp.int32)
    return jnp.sum(jnp.where(indices[:, None] == places[None, :], table[None, :], 0.0), axis=1)


def turn_kernel(rows, out):
    out[...] = rows[...].T


def turned(amplitudes):
    rows, depth = amplitudes.shape
    return pl.pallas_call(
        turn_kernel,
        grid=(depth // DEPTH,),
        in_specs=[pl.BlockSpec((rows, DEPTH), lambda k: (0, k))],
        out_specs=pl.BlockSpec((DEPTH, rows), lambda k: (k, 0)),
        out_shape=jax.ShapeDtypeStruct((depth, rows), amplitudes.dtype),
        compiler_params=pltpu.CompilerParams(vmem_limit_bytes=8 * 1024 * 1024),
        cost_estimate=pl.CostEstimate(flops=0, bytes_accessed=0, transcendentals=0),
    )(amplitudes)


def accumulate(total, blocks, amplitudes):
    step = pl.program_id(0)
    stacked = jnp.concatenate([block[...] for block in blocks], axis=0)
    for half, rows in enumerate(amplitudes):
        count = rows.shape[1]
        columns = slice(half * count, (half + 1) * count)
        part = jnp.dot(stacked, rows[...], preferred_element_type=jnp.float32)

        @pl.when(step == 0)
        def _():
            total[:, columns] = part

        @pl.when(step > 0)
        def _():
            total[:, columns] += part


def product_kernel(*refs):
    *blocks, own, other, total = refs
    accumulate(total, blocks, (own, other))


def coded(sums):
    largest = jnp.maximum(jnp.max(jnp.abs(sums), axis=1, keepdims=True), SMALLEST)
    power = jnp.clip(jnp.floor(jnp.log2(largest)) + 1.0, -126.0, 126.0)
    scale = jnp.exp2(-power)
    part = jnp.ceil(largest * scale * 256.0)
    whole = jnp.round(sums * scale * (256.0 * UNITS / part))
    place = lax.broadcasted_iota(jnp.int32, (16, 128), 1)
    note = jnp.zeros((16, 128), jnp.float32)
    pieces = []
    for g in range(sums.shape[0] // 16):
        these = slice(g * 16, (g + 1) * 16)
        note = jnp.where(place == 2 * g, power[these], jnp.where(place == 2 * g + 1, part[these], note))
        pieces.append(whole[these])
    return jnp.concatenate([*pieces, note], axis=1).astype(jnp.int32).astype(jnp.int16)


def coded_shape(rows, width):
    return (16, rows // 16 * width + 128)


def decoded(share, width):
    count = share.shape[1] // width
    rows = []
    for g in range(count):
        note = share[:, count * width :].astype(jnp.float32)
        power, part = note[:, 2 * g : 2 * g + 1], note[:, 2 * g + 1 : 2 * g + 2]
        scale = part * (1.0 / (256.0 * UNITS)) * jnp.exp2(power)
        rows.append(share[:, g * width : (g + 1) * width].astype(jnp.float32) * scale)
    return jnp.concatenate(rows, axis=0)


def finish_kernel(counts, spots, *refs):
    last = counts[-1]
    blocks, (own, other), earlier = refs[:last], refs[last : last + 2], refs[last + 2 : -6]
    kept, up, down, far, total, ordered = refs[-6:]
    accumulate(total, blocks, (own, other))

    @pl.when(pl.program_id(0) == pl.num_programs(0) - 1)
    def _():
        row, z = lax.axis_index("row"), lax.axis_index("col") // 2
        x, y, core = row // (2 * YS), row // 2 % YS, row % 2
        n = ordered.shape[1]
        i = 0
        for count, sums in zip(counts, (*earlier, total)):
            for j in range(count):
                (x0, y0), (x1, y1) = spots[0][i], spots[1][i]
                from_x = jnp.where(core == 0, x ^ x0, x ^ x1)
                from_y = jnp.where(core == 0, (y + YS - y0) % YS, (y + YS - y1) % YS)
                ordered[(from_x * YS + from_y + ZS - z) % ZS] = sums[j * n : (j + 1) * n, :]
                i += 1
        for place, step in enumerate((0, 2, 6)):
            kept[place] = ordered[step]
        up[0], up[1] = coded(ordered[1]), coded(ordered[3])
        down[0], down[1] = coded(ordered[7]), coded(ordered[5])
        far[...] = coded(ordered[4])


def pass_kernel(kept, from_below, from_above, from_far, up, down):
    width = kept.shape[2]
    even = (lax.axis_index("col") // 2) % 2 == 0
    far = decoded(from_far[...], width)
    up[...] = coded(kept[1] + decoded(from_below[1], width) + jnp.where(even, far, 0.0))
    down[...] = coded(kept[2] + decoded(from_above[1], width) + jnp.where(even, 0.0, far))


def along_z(sums, even, odd):
    pairs = [(a * 2 + b, (a + (odd if a % 2 else even)) % ZS * 2 + b) for a in range(ZS) for b in range(2)]
    return lax.ppermute(sums, "col", pairs)


def sum_along_z(kept, up, down, far):
    _, n, width = kept.shape
    from_far = along_z(far, 2, -2)
    from_below, from_above = along_z(up, 1, 1), along_z(down, -1, -1)
    shape = jax.ShapeDtypeStruct(coded_shape(n, width), jnp.int16)
    up, down = pl.pallas_call(
        pass_kernel,
        out_shape=[shape, shape],
        compiler_params=pltpu.CompilerParams(vmem_limit_bytes=12 * 1024 * 1024),
        cost_estimate=pl.CostEstimate(flops=0, bytes_accessed=0, transcendentals=0),
    )(kept, from_below, from_above, from_far)
    near = (from_below[0], from_above[0], along_z(up, 2, 2), along_z(down, -2, -2))
    return kept[0] + sum(decoded(share, width) for share in near)


def multiply(kernel, blocks, own, other, earlier, outs, scratch, step=DEPTH, room=16):
    n, depth = blocks[0].shape
    rows = own.shape[1]
    whole = lambda shape: pl.BlockSpec(shape, lambda k: (0,) * len(shape))
    return pl.pallas_call(
        kernel,
        grid=(depth // step,),
        in_specs=[pl.BlockSpec((n, step), lambda k: (0, k))] * len(blocks)
        + [pl.BlockSpec((step, rows), lambda k: (k, 0))] * 2
        + [whole(sums.shape) for sums in earlier],
        out_specs=[whole(out.shape) for out in outs],
        out_shape=list(outs),
        scratch_shapes=scratch,
        compiler_params=pltpu.CompilerParams(vmem_limit_bytes=room * 1024 * 1024),
        cost_estimate=pl.CostEstimate(flops=0, bytes_accessed=0, transcendentals=0),
    )(*blocks, own, other, *earlier)


def sums_of(blocks, own, other):
    n, width = blocks[0].shape[0], 2 * own.shape[1]
    out = jax.ShapeDtypeStruct((len(blocks) * n, width), jnp.float32)
    return multiply(product_kernel, blocks, own, other, (), (out,), ())[0]


def last_sums(blocks, own, other, earlier, spots, groups):
    n, width = blocks[0].shape[0], 2 * own.shape[1]
    counts = tuple(b - a for a, b in groups)
    kernel = functools.partial(finish_kernel, counts, spots)
    scratch = [pltpu.VMEM((len(blocks) * n, width), jnp.float32), pltpu.VMEM((8, n, width), jnp.float32)]
    one = coded_shape(n, width)
    pair = jax.ShapeDtypeStruct((2, *one), jnp.int16)
    outs = (jax.ShapeDtypeStruct((3, n, width), jnp.float32), pair, pair, jax.ShapeDtypeStruct(one, jnp.int16))
    return multiply(kernel, blocks, own, other, earlier, outs, scratch, LAST_DEPTH, 28)


def after(value, *others):
    return lax.optimization_barrier((value, *others))[0]


def partials(rows, amplitudes):
    done = {"other": turned(lax.ppermute(amplitudes, "row", PARTNER)), "own": turned(amplitudes)}
    held, earlier, start = [], [], 0
    for n, *_ in SLICES:
        held.append([lax.slice_in_dim(rows, start, start + n, axis=0)])
        earlier.append([])
        start += n
    for name, needs in ORDER:
        s, i = int(name[1]), int(name[2])
        n, sources, first, second = SLICES[s]
        if name[0] == "s":
            block = after(held[s][sources[i]], *(done[need] for need in needs))
            done[name] = lax.ppermute(block, "row", row_perm((first[i], second[i])))
            held[s].append(done[name])
            continue
        a, b = GROUPS[s][i]
        blocks = held[s][a:b]
        blocks[0] = after(blocks[0], *(done[need] for need in needs))
        if b < 8:
            done[name] = sums_of(blocks, done["own"], done["other"])
            earlier[s].append(done[name])
        else:
            spots = (places(sources, first), places(sources, second))
            done[name] = last_sums(blocks, done["own"], done["other"], earlier[s], spots, GROUPS[s])
            return done[name]


def on_device(amplitudes, integrals, pair_first, pair_second, occ_energy, vir_energy):
    local_rows = amplitudes.shape[0]
    row, col = lax.axis_index("row"), lax.axis_index("col")
    core, h = row % 2, col % 2
    same = h == core
    mine = sum_along_z(*partials(integrals.T, amplitudes))
    own, theirs = mine[:, :local_rows], mine[:, local_rows:]
    ladder = lax.ppermute(jnp.where(same, theirs, own), ("row", "col"), swap_perm(1)) + lax.ppermute(
        jnp.where(same, own, theirs), ("row", "col"), swap_perm(0)
    )

    nocc_count = occ_energy.shape[0]
    pair_rows = row * local_rows + jnp.arange(local_rows, dtype=jnp.int32)
    first_occ = lookup(pair_rows // nocc_count, occ_energy)
    second_occ = lookup(pair_rows % nocc_count, occ_energy)
    first_vir = lookup(pair_first, vir_energy)
    second_vir = lookup(pair_second, vir_energy)
    denominator = (
        first_occ[None, :] + second_occ[None, :] - first_vir[:, None] - second_vir[:, None]
    )
    return (ladder / denominator).astype(jnp.bfloat16).T


def solution(mesh):
    placed = (P("row", "col"), P("col", "row"), P("col"), P("col"), P(), P())
    return jax.shard_map(
        on_device, mesh=mesh, in_specs=placed, out_specs=P("row", "col"), check_vma=False
    )
```
